32 devices in a mesh: dp: 4 (over y, x), tensor: 8 (over z, core).
Axes of the slice: x: 2, y: 2, z: 4, core: 2. Of those that a mesh axis runs over, the one named last changes fastest.
Arguments:
- acts: bfloat16 [4096, 28672], P('dp', 'tensor'), may hold values from -6 to 6
- out_grads: bfloat16 [4096, 8192], P('dp', 'tensor'), may hold values from -4 to 4
- proj_in: bfloat16 [28672, 64], P('tensor'), may hold values from -0.03125 to 0.03125
- proj_out: bfloat16 [8192, 64], P('tensor'), may hold values from -0.0625 to 0.0625
- doc_lengths: int32 [4, 4], P('dp'), may hold values from 1 to 512, 1024 in all within a row
- owner_map: int32 [4, 4], P('dp'), may hold values from 0 to 3, each once within a row
Outputs:
- doc_grads: float32 [16, 4096], P('dp', 'tensor')
The draws below stay inside these ranges and needn't reach their ends.
Inputs may be any that keep to these rules, and one draw needn't show every extreme that they name: `doc_lengths`: each row sums to 1024 and its largest entry is 512. `owner_map`: each row is a permutation of the owners.
All inputs are finite; a program needn't handle non-finite values.
Results may differ from the reference program's by a relative error of at most 0.0003.
Values may be sent and summed in bfloat16 or wider, within the bound.
No kernel may reach another device: no remote copies, remote signals or barrier semaphores. Data moves between devices by JAX's collectives and lax.ppermute only.
A program may use at most 64 MiB of HBM per device.

```python
import math
import jax
import jax.numpy as jnp
import numpy as np
from jax import lax

D = 8192
FF = 28672
R = 64
LEN = 1024
SEQS = 4
TOKENS = 4096
MOST = 512
N_DP = 4


def level_of(stream_key, dims, split, smallest, high):
    gain = 1.0
    for axis_at, shards_of in split:
        heights = jax.random.uniform(jax.random.fold_in(jax.random.fold_in(stream_key, 6), axis_at), (shards_of,), jnp.float32, smallest / len(split), high / len(split))
        gain = gain * jnp.repeat(jnp.exp(heights), dims[axis_at] // shards_of).reshape((-1,) + (1,) * (len(dims) - 1 - axis_at))
    return gain


def split_up(amount, total, reach, skew):
    weights = [(1 << 20) // math.isqrt(rank ** skew) + 1 for rank in range(2, amount + 1)]
    surplus, given = total - reach - (amount - 1), [1] * (amount - 1)
    while surplus > 0:
        candidates = [i for i in range(amount - 1) if given[i] < reach]
        pool, budget = sum([weights[i] for i in candidates]), surplus
        for i in candidates:
            addition = min(reach - given[i], max(1, budget * weights[i] // pool), surplus)
            given[i] = given[i] + addition
            surplus = surplus - addition
    return np.array([reach] + given)


def uneven(stream_key, amount, total, bound, skew):
    if amount == 2:
        one = jax.random.randint(stream_key, (), max(1, total - bound), min(bound, total - 1) + 1)
        return jnp.stack([one, total - one])
    tallies = jnp.asarray(split_up(amount, total, bound, skew), jnp.int32)
    twos = (amount - 1) // 2
    source_of, sink = tallies[1:1 + 2 * twos:2], tallies[2:2 + 2 * twos:2]
    margin = jnp.minimum(source_of - 1, bound - sink)
    passed = jax.random.randint(jax.random.fold_in(stream_key, 1), (twos,), 0, 1 << 20) % (margin + 1)
    tallies = tallies.at[1:1 + 2 * twos:2].set(source_of - passed).at[2:2 + 2 * twos:2].set(sink + passed)
    return tallies[jax.random.permutation(jax.random.fold_in(stream_key, 2), amount)]


def scatter_about(key, dims, spread, most, pieces=(), held_as=jnp.bfloat16):
    loudness = level_of(key, dims, pieces, -0.22, 0.18) if pieces else 1.0
    result = jax.random.normal(key, dims, jnp.float32) * spread * loudness
    return jnp.minimum(jnp.maximum(result, -most), most).astype(held_as)


def setup_inputs(seed: int = 0) -> dict:
    splits = jax.random.split(jax.random.key(seed), 7)
    return {
        "acts": scatter_about(splits[0], (TOKENS, FF), 1.0, 6.0, ((0, 4), (1, 8))),
        "out_grads": scatter_about(splits[1], (TOKENS, D), 0.25, 4.0, ((0, 4), (1, 8))),
        "proj_in": scatter_about(splits[2], (FF, R), FF ** -0.5, 0.03125, ((0, 8),)),
        "proj_out": scatter_about(splits[3], (D, R), D ** -0.5, 0.0625, ((0, 8),)),
        "doc_lengths": jax.vmap(lambda own: uneven(own, N_DP, LEN, MOST, 2))(jax.random.split(splits[4], SEQS)).reshape((SEQS, N_DP)).astype(jnp.int32),
        "owner_map": jax.vmap(lambda own: jax.random.permutation(own, N_DP))(jax.random.split(splits[5], SEQS)).reshape((SEQS, N_DP)).astype(jnp.int32),
    }


def reference(acts, out_grads, proj_in, proj_out, doc_lengths, owner_map):
    proj_rank = proj_in.shape[1]
    hidden_seq = acts.reshape(N_DP, LEN, FF)
    grads_seq = out_grads.reshape(N_DP, LEN, D)

    def per_sequence(inputs):
        hidden_rows, grad_rows, doc_len, doc_owner = inputs
        in_side = jnp.dot(hidden_rows, proj_in, preferred_element_type=jnp.float32)
        out_side = jnp.dot(grad_rows, proj_out, preferred_element_type=jnp.float32)
        outer_rows = (out_side[:, :, None] * in_side[:, None, :]).reshape(LEN, proj_rank * proj_rank)
        doc_end = jnp.cumsum(doc_len).astype(jnp.int32)
        doc_start = doc_end - doc_len
        position = jnp.arange(LEN, dtype=jnp.int32)
        member = ((position[:, None] >= doc_start[None, :]) & (position[:, None] < doc_end[None, :])).astype(jnp.float32)
        per_doc = jnp.dot(member.T, outer_rows, precision=lax.Precision.HIGHEST)
        routing = (doc_owner[None, :] == jnp.arange(N_DP, dtype=jnp.int32)[:, None]).astype(jnp.float32)
        return jnp.dot(routing, per_doc, precision=lax.Precision.HIGHEST)

    stacked = lax.map(per_sequence, (hidden_seq, grads_seq, doc_lengths, owner_map))
    return jnp.transpose(stacked, (1, 0, 2)).reshape(N_DP * N_DP, proj_rank * proj_rank)
```

```python
import functools
import math
import jax
import jax.numpy as jnp
from jax import lax
from jax.experimental import pallas as pl
from jax.experimental.pallas import tpu as pltpu
from jax.sharding import PartitionSpec as P

NT = (((1,), (1,)), ((), ()))


def project(place, acts_hbm, grads_hbm, in_hbm, out_hbm, kept, sent, held, weights, w_sems, sems):
    rank = in_hbm.shape[0]
    chunks, length, depth = held.shape
    hidden, width = acts_hbm.shape[1], grads_hbm.shape[1]
    half = length // 2
    rows = half // 2
    ahead = min(4, chunks)

    def copy(i):
        if i * depth < width:
            source = grads_hbm.at[:, pl.ds(i * depth, depth)]
        else:
            source = acts_hbm.at[:, pl.ds(i * depth - width, depth)]
        return pltpu.make_async_copy(source, held.at[i], sems.at[i])

    loads = (
        pltpu.make_async_copy(
            out_hbm, weights.at[pl.ds(rank, rank), pl.ds(0, width)], w_sems.at[0]
        ),
        pltpu.make_async_copy(
            in_hbm, weights.at[pl.ds(0, rank), pl.ds(width, hidden)], w_sems.at[1]
        ),
    )
    for load in loads:
        load.start()
    for i in range(ahead):
        copy(i).start()
    weights[pl.ds(0, rank), pl.ds(0, width)] = jnp.zeros((rank, width), weights.dtype)
    weights[pl.ds(rank, rank), pl.ds(width, hidden)] = jnp.zeros((rank, hidden), weights.dtype)
    for load in loads:
        load.wait()
    core = place[0]
    for i in range(chunks):
        copy(i).wait()
        if i + ahead < chunks:
            copy(i + ahead).start()
        block = weights[:, i * depth : (i + 1) * depth]
        for out, base in ((sent, (1 - core) * half), (kept, core * half)):
            for at in range(0, half, rows):
                part = held[i, pl.ds(pl.multiple_of(base + at, rows), rows), :]
                term = lax.dot_general(part, block, NT, preferred_element_type=jnp.float32)
                if i:
                    out[pl.ds(at, rows), :] += term
                else:
                    out[pl.ds(at, rows), :] = term


def outer(doc_len, doc_owner, place, parts, out, turned, picked):
    slots, tokens, lanes = parts.shape
    docs = doc_len.shape[1]
    owners = out.shape[0]
    rank = lanes // 2
    half = rank // 2
    rows = parts[0]
    for i in range(1, slots):
        rows = rows + parts[i]
    turned[...] = rows.T
    lane = lax.broadcasted_iota(jnp.int32, rows.shape, 1)
    left = jnp.where(lane < rank, rows, 0.0)
    right = jnp.where(lane < rank, 0.0, pltpu.roll(rows, rank, 1))
    even = turned[pl.ds(rank, half, stride=2), :]
    odd = turned[pl.ds(rank + 1, half, stride=2), :]
    at = place[1] + lax.broadcasted_iota(jnp.int32, even.shape, 1)
    starts = []
    start = jnp.int32(0)
    for k in range(docs):
        starts.append(start)
        start = start + doc_len[0, k]
    for o in range(owners):
        first, last = jnp.int32(0), jnp.int32(0)
        for k in range(docs):
            mine = doc_owner[0, k] == o
            first = jnp.where(mine, starts[k], first)
            last = jnp.where(mine, starts[k] + doc_len[0, k], last)
        live = (at >= first) & (at < last)
        picked[0, pl.ds(o * half, half), :] = jnp.where(live, even, 0.0)
        picked[1, pl.ds(o * half, half), :] = jnp.where(live, odd, 0.0)
    dot = functools.partial(
        jnp.dot, precision=lax.Precision.HIGHEST, preferred_element_type=jnp.float32
    )
    grads = dot(picked[0], left) + dot(picked[1], right)
    out[...] = grads.reshape(out.shape)


def collect(parts, out):
    seqs, width = out.shape
    lanes = parts.shape[1]
    blocks = width // lanes
    terms = parts.shape[0] // (seqs * blocks)
    for s in range(seqs):
        for c in range(blocks):
            block = parts[pl.ds(s * terms * blocks + c, terms, stride=blocks), :]
            out[pl.ds(s, 1), pl.ds(c * lanes, lanes)] = jnp.sum(block, axis=0, keepdims=True)


def on_device(acts, out_grads, proj_in, proj_out, doc_lengths, owner_map):
    owners = lax.axis_size("dp")
    split = lax.axis_size("tensor")
    length, hidden = acts.shape
    width = out_grads.shape[1]
    rank = proj_in.shape[1]
    lanes = 2 * rank
    depth = math.gcd(512, math.gcd(hidden, width))
    pairs = split // 2
    tokens = length // split
    vmem = pl.BlockSpec(memory_space=pltpu.VMEM)
    smem = pl.BlockSpec(memory_space=pltpu.SMEM)
    hbm = pl.BlockSpec(memory_space=pl.ANY)

    at = lax.axis_index("tensor")
    core, pair = at % 2, at // 2
    place = jnp.stack([core, core * (length // 2) + pair * tokens]).astype(jnp.int32)
    half = pltpu.VMEM((length // 2, lanes), jnp.float32)
    kept, sent = pl.pallas_call(
        project,
        out_shape=(half, half),
        in_specs=[smem] + [hbm] * 4,
        out_specs=(vmem, vmem),
        scratch_shapes=[
            pltpu.VMEM(((hidden + width) // depth, length, depth), acts.dtype),
            pltpu.VMEM((lanes, hidden + width), proj_in.dtype),
            pltpu.SemaphoreType.DMA((2,)),
            pltpu.SemaphoreType.DMA(((hidden + width) // depth,)),
        ],
        compiler_params=pltpu.CompilerParams(vmem_limit_bytes=56 << 20),
    )(place, acts, out_grads, proj_in.T, proj_out.T)
    got = lax.ppermute(sent, "tensor", [(i, i ^ 1) for i in range(split)])
    halves = (kept + got).reshape(pairs, tokens, lanes)
    parts = jnp.stack(
        [lax.dynamic_index_in_dim(halves, pair, 0, keepdims=False)]
        + [
            lax.ppermute(
                lax.dynamic_index_in_dim(halves, pair ^ m, 0, keepdims=False),
                "tensor",
                [(i, i ^ (2 * m)) for i in range(split)],
            )
            for m in range(1, pairs)
        ]
    )
    grads = pl.pallas_call(
        outer,
        out_shape=pltpu.VMEM((owners, rank // 2, lanes), jnp.float32),
        in_specs=[smem, smem, smem, vmem],
        out_specs=vmem,
        scratch_shapes=[
            pltpu.VMEM((lanes, tokens), jnp.float32),
            pltpu.VMEM((2, owners * rank // 2, tokens), jnp.float32),
        ],
        compiler_params=pltpu.CompilerParams(vmem_limit_bytes=8 << 20),
    )(doc_lengths, owner_map, place, parts)
    got = lax.all_to_all(
        grads.reshape(owners * rank // 2, lanes), ("dp", "tensor"), 0, 0, tiled=True
    )
    return pl.pallas_call(
        collect,
        out_shape=jax.ShapeDtypeStruct((owners, rank * rank // split), jnp.float32),
        in_specs=[vmem],
        out_specs=vmem,
        compiler_params=pltpu.CompilerParams(vmem_limit_bytes=8 << 20),
    )(got)


def solution(mesh):
    in_specs = (
        P("dp", "tensor"),
        P("dp", "tensor"),
        P("tensor", None),
        P("tensor", None),
        P("dp", None),
        P("dp", None),
    )
    out_specs = P("dp", "tensor")
    return jax.shard_map(
        on_device, mesh=mesh, in_specs=in_specs, out_specs=out_specs, check_vma=False
    )
```

```python
import functools
import math
import jax
import jax.numpy as jnp
from jax import lax
from jax.experimental import pallas as pl
from jax.experimental.pallas import tpu as pltpu
from jax.sharding import PartitionSpec as P

NT = (((1,), (1,)), ((), ()))
TOP = 32767.0


def project(acts_hbm, grads_hbm, in_hbm, out_hbm, sums, held, weights, w_sems, sems):
    rank = in_hbm.shape[0]
    chunks, length, depth = held.shape
    hidden, width = acts_hbm.shape[1], grads_hbm.shape[1]
    rows = length // 4
    ahead = min(5, chunks)

    def copy(i):
        if i * depth < width:
            source = grads_hbm.at[:, pl.ds(i * depth, depth)]
        else:
            source = acts_hbm.at[:, pl.ds(i * depth - width, depth)]
        return pltpu.make_async_copy(source, held.at[i], sems.at[i])

    loads = (
        pltpu.make_async_copy(
            out_hbm, weights.at[pl.ds(rank, rank), pl.ds(0, width)], w_sems.at[0]
        ),
        pltpu.make_async_copy(
            in_hbm, weights.at[pl.ds(0, rank), pl.ds(width, hidden)], w_sems.at[1]
        ),
    )
    loads[0].start()
    copy(0).start()
    loads[1].start()
    for i in range(1, ahead):
        copy(i).start()
    weights[pl.ds(0, rank), pl.ds(0, width)] = jnp.zeros((rank, width), weights.dtype)
    weights[pl.ds(rank, rank), pl.ds(width, hidden)] = jnp.zeros((rank, hidden), weights.dtype)
    loads[0].wait()
    for i in range(chunks):
        if i * depth == width:
            loads[1].wait()
        copy(i).wait()
        if i + ahead < chunks:
            copy(i + ahead).start()
        block = weights[:, i * depth : (i + 1) * depth]
        for at in range(0, length, rows):
            part = held[i, pl.ds(at, rows), :]
            term = lax.dot_general(part, block, NT, preferred_element_type=jnp.float32)
            if i:
                sums[pl.ds(at, rows), :] += term
            else:
                sums[pl.ds(at, rows), :] = term


def code(at, sums, got, own, *sent):
    lanes, tokens = own.shape
    rank = lanes // 2
    pair = at[0] // 2
    kept = lax.rem(at[0], 2) * got.shape[0]

    def block(m):
        start = pl.multiple_of((pair ^ m) * tokens, tokens)
        mine = pl.ds(pl.multiple_of(kept + start, tokens), tokens)
        return (sums[mine, :] + got[pl.ds(start, tokens), :]).T

    own[...] = block(0)
    for m, out in enumerate(sent, 1):
        value = block(m)
        powers = []
        for side in range(2):
            part = value[side * rank : (side + 1) * rank]
            largest = jnp.max(jnp.abs(part), axis=0, keepdims=True)
            power = jnp.ceil(jnp.log2(jnp.maximum(largest, 1e-30)))
            steps = jnp.round(part * jnp.exp2(15.0 - power))
            steps = jnp.minimum(jnp.maximum(steps, -TOP), TOP).astype(jnp.int32)
            out[pl.ds(side * rank, rank), :] = steps.astype(jnp.int16)
            powers.append(power)
        row = lax.broadcasted_iota(jnp.int32, (out.shape[0] - lanes, tokens), 0)
        power = jnp.where(row == 0, powers[0], powers[1]).astype(jnp.int32)
        out[pl.ds(lanes, row.shape[0]), :] = power.astype(jnp.int16)


def outer(doc_len, doc_owner, at, own, *refs):
    *parts, out, sums, picked, other = refs
    lanes, tokens = own.shape
    docs = doc_len.shape[1]
    owners = out.shape[0]
    rank = lanes // 2
    half = rank // 2
    sides = [own[pl.ds(0, rank), :], own[pl.ds(rank, rank), :]]
    for part in parts:
        powers = part[pl.ds(lanes, part.shape[0] - lanes), :].astype(jnp.int32)
        scales = jnp.exp2(powers.astype(jnp.float32) - 15.0)
        for side in range(2):
            steps = part[pl.ds(side * rank, rank), :].astype(jnp.int32).astype(jnp.float32)
            sides[side] = sides[side] + steps * scales[side : side + 1]
    sums[...] = sides[1]
    zero = jnp.zeros((rank, tokens), jnp.float32)
    other[0, pl.ds(0, rank), :] = sides[0]
    other[0, pl.ds(rank, rank), :] = zero
    other[1, pl.ds(0, rank), :] = zero
    other[1, pl.ds(rank, rank), :] = sides[0]
    even = sums[pl.ds(0, half, stride=2), :]
    odd = sums[pl.ds(1, half, stride=2), :]
    start = lax.rem(at[0], 2) * (tokens * (len(parts) + 1)) + at[0] // 2 * tokens
    place = start + lax.broadcasted_iota(jnp.int32, even.shape, 1)
    starts = []
    start = jnp.int32(0)
    for k in range(docs):
        starts.append(start)
        start = start + doc_len[0, k]
    for o in range(owners):
        first, last = jnp.int32(0), jnp.int32(0)
        for k in range(docs):
            mine = doc_owner[0, k] == o
            first = jnp.where(mine, starts[k], first)
            last = jnp.where(mine, starts[k] + doc_len[0, k], last)
        live = (place >= first) & (place < last)
        picked[0, pl.ds(o * half, half), :] = jnp.where(live, even, 0.0)
        picked[1, pl.ds(o * half, half), :] = jnp.where(live, odd, 0.0)
    dot = functools.partial(
        lax.dot_general,
        dimension_numbers=NT,
        precision=lax.Precision.HIGHEST,
        preferred_element_type=jnp.float32,
    )
    grads = dot(picked[0], other[0]) + dot(picked[1], other[1])
    out[...] = grads.reshape(out.shape)


def collect(parts, out):
    seqs, width = out.shape
    lanes = parts.shape[1]
    blocks = width // lanes
    terms = parts.shape[0] // (seqs * blocks)
    for s in range(seqs):
        for c in range(blocks):
            block = parts[pl.ds(s * terms * blocks + c, terms, stride=blocks), :]
            out[pl.ds(s, 1), pl.ds(c * lanes, lanes)] = jnp.sum(block, axis=0, keepdims=True)


def on_device(acts, out_grads, proj_in, proj_out, doc_lengths, owner_map):
    owners = lax.axis_size("dp")
    split = lax.axis_size("tensor")
    length, hidden = acts.shape
    width = out_grads.shape[1]
    rank = proj_in.shape[1]
    lanes = 2 * rank
    depth = math.gcd(512, math.gcd(hidden, width))
    chunks = (hidden + width) // depth
    pairs = split // 2
    tokens = length // split
    half = length // 2
    vmem = pl.BlockSpec(memory_space=pltpu.VMEM)
    smem = pl.BlockSpec(memory_space=pltpu.SMEM)
    hbm = pl.BlockSpec(memory_space=pl.ANY)
    small = pltpu.CompilerParams(vmem_limit_bytes=8 << 20)

    at = lax.axis_index("tensor").astype(jnp.int32).reshape(1)
    sums = pl.pallas_call(
        project,
        out_shape=pltpu.VMEM((length, lanes), jnp.float32),
        in_specs=[hbm] * 4,
        out_specs=vmem,
        scratch_shapes=[
            pltpu.VMEM((chunks, length, depth), acts.dtype),
            pltpu.VMEM((lanes, hidden + width), proj_in.dtype),
            pltpu.SemaphoreType.DMA((2,)),
            pltpu.SemaphoreType.DMA((chunks,)),
        ],
        compiler_params=pltpu.CompilerParams(vmem_limit_bytes=56 << 20),
    )(acts, out_grads, proj_in.T, proj_out.T)
    sent = lax.dynamic_slice_in_dim(sums, (1 - at[0] % 2) * half, half, 0)
    got = lax.ppermute(sent, "tensor", [(i, i ^ 1) for i in range(split)])
    own, *coded = pl.pallas_call(
        code,
        out_shape=(pltpu.VMEM((lanes, tokens), jnp.float32),)
        + (pltpu.VMEM((lanes + 16, tokens), jnp.int16),) * (pairs - 1),
        in_specs=[smem, vmem, vmem],
        out_specs=(vmem,) * pairs,
        compiler_params=small,
    )(at, sums, got)
    parts = [None] * (pairs - 1)
    for m in range(1, pairs):
        parts[m - 1] = lax.ppermute(
            coded[m - 1], "tensor", [(i, i ^ (2 * m)) for i in range(split)]
        )
    grads = pl.pallas_call(
        outer,
        out_shape=pltpu.VMEM((owners, rank // 2, lanes), jnp.float32),
        in_specs=[smem] * 3 + [vmem] * pairs,
        out_specs=vmem,
        scratch_shapes=[
            pltpu.VMEM((rank, tokens), jnp.float32),
            pltpu.VMEM((2, owners * rank // 2, tokens), jnp.float32),
            pltpu.VMEM((2, lanes, tokens), jnp.float32),
        ],
        compiler_params=small,
    )(doc_lengths, owner_map, at, own, *parts)
    got = lax.all_to_all(
        grads.reshape(owners * rank // 2, lanes), ("dp", "tensor"), 0, 0, tiled=True
    )
    return pl.pallas_call(
        collect,
        out_shape=jax.ShapeDtypeStruct((owners, rank * rank // split), jnp.float32),
        in_specs=[vmem],
        out_specs=vmem,
        compiler_params=small,
    )(got)


def solution(mesh):
    in_specs = (
        P("dp", "tensor"),
        P("dp", "tensor"),
        P("tensor", None),
        P("tensor", None),
        P("dp", None),
        P("dp", None),
    )
    out_specs = P("dp", "tensor")
    return jax.shard_map(
        on_device, mesh=mesh, in_specs=in_specs, out_specs=out_specs, check_vma=False
    )
```

```python
import functools
import math
import jax
import jax.numpy as jnp
from jax import lax
from jax.experimental import pallas as pl
from jax.experimental.pallas import tpu as pltpu
from jax.sharding import PartitionSpec as P

NT = (((1,), (1,)), ((), ()))
TOP = 32767.0


def project(acts_hbm, grads_hbm, in_hbm, out_hbm, sums, held, weights, w_sems, sems):
    rank = in_hbm.shape[0]
    chunks, length, depth = held.shape
    hidden, width = acts_hbm.shape[1], grads_hbm.shape[1]
    rows = length // 4
    ahead = min(5, chunks)

    def copy(i):
        if i * depth < width:
            source = grads_hbm.at[:, pl.ds(i * depth, depth)]
        else:
            source = acts_hbm.at[:, pl.ds(i * depth - width, depth)]
        return pltpu.make_async_copy(source, held.at[i], sems.at[i])

    loads = (
        pltpu.make_async_copy(
            out_hbm, weights.at[pl.ds(rank, rank), pl.ds(0, width)], w_sems.at[0]
        ),
        pltpu.make_async_copy(
            in_hbm, weights.at[pl.ds(0, rank), pl.ds(width, hidden)], w_sems.at[1]
        ),
    )
    loads[0].start()
    copy(0).start()
    loads[1].start()
    for i in range(1, ahead):
        copy(i).start()
    weights[pl.ds(0, rank), pl.ds(0, width)] = jnp.zeros((rank, width), weights.dtype)
    weights[pl.ds(rank, rank), pl.ds(width, hidden)] = jnp.zeros((rank, hidden), weights.dtype)
    loads[0].wait()
    for i in range(chunks):
        if i * depth == width:
            loads[1].wait()
        copy(i).wait()
        if i + ahead < chunks:
            copy(i + ahead).start()
        block = weights[:, i * depth : (i + 1) * depth]
        for at in range(0, length, rows):
            part = held[i, pl.ds(at, rows), :]
            term = lax.dot_general(part, block, NT, preferred_element_type=jnp.float32)
            if i:
                sums[pl.ds(at, rows), :] += term
            else:
                sums[pl.ds(at, rows), :] = term


def code(order, at, sums, got, own, *sent):
    lanes, tokens = own.shape
    rank = lanes // 2
    pair = at[0] // 2
    kept = lax.rem(at[0], 2) * got.shape[0]

    def block(m):
        start = pl.multiple_of((pair ^ m) * tokens, tokens)
        mine = pl.ds(pl.multiple_of(kept + start, tokens), tokens)
        return (sums[mine, :] + got[pl.ds(start, tokens), :]).T

    own[...] = block(0)
    for m, out in zip(order, sent):
        value = block(m)
        powers = []
        for side in range(2):
            part = value[side * rank : (side + 1) * rank]
            largest = jnp.max(jnp.abs(part), axis=0, keepdims=True)
            power = jnp.ceil(jnp.log2(jnp.maximum(largest, 1e-30)))
            steps = jnp.round(part * jnp.exp2(15.0 - power))
            steps = jnp.minimum(jnp.maximum(steps, -TOP), TOP).astype(jnp.int32)
            out[pl.ds(side * rank, rank), :] = steps.astype(jnp.int16)
            powers.append(power)
        row = lax.broadcasted_iota(jnp.int32, (out.shape[0] - lanes, tokens), 0)
        power = jnp.where(row == 0, powers[0], powers[1]).astype(jnp.int32)
        out[pl.ds(lanes, row.shape[0]), :] = power.astype(jnp.int16)


def members(pairs, doc_len, doc_owner, at, lives):
    owners, tokens = lives.shape
    docs = doc_len.shape[1]
    core, pair = lax.rem(at[0], 2), at[0] // 2
    first_token = (core * pairs + pair) * tokens
    place = first_token + lax.broadcasted_iota(jnp.int32, (1, tokens), 1)
    starts = []
    start = jnp.int32(0)
    for k in range(docs):
        starts.append(start)
        start = start + doc_len[0, k]
    for o in range(owners):
        first, last = jnp.int32(0), jnp.int32(0)
        for k in range(docs):
            mine = doc_owner[0, k] == o
            first = jnp.where(mine, starts[k], first)
            last = jnp.where(mine, starts[k] + doc_len[0, k], last)
        lives[pl.ds(o, 1), :] = ((place >= first) & (place < last)).astype(jnp.float32)


def cut(value):
    high = value.astype(jnp.bfloat16)
    return high, (value - high.astype(jnp.float32)).astype(jnp.bfloat16)


def outer(lives, own, *refs):
    *parts, out, sums, picked, other = refs
    lanes, tokens = own.shape
    owners = out.shape[0]
    rank = lanes // 2
    half = rank // 2
    sides = [own[pl.ds(0, rank), :], own[pl.ds(rank, rank), :]]
    for part in parts:
        powers = part[pl.ds(lanes, part.shape[0] - lanes), :].astype(jnp.int32)
        scales = jnp.exp2(powers.astype(jnp.float32) - 15.0)
        for side in range(2):
            steps = part[pl.ds(side * rank, rank), :].astype(jnp.int32).astype(jnp.float32)
            sides[side] = sides[side] + steps * scales[side : side + 1]
    sums[...] = sides[1]
    high, low = cut(sides[0])
    other[...] = jnp.zeros(other.shape, other.dtype)
    for side in range(2):
        for term, piece in enumerate((high, low, high)):
            columns = pl.ds((2 * term + side) * tokens, tokens)
            other[pl.ds(side * rank, rank), columns] = piece
    high, low = zip(*(cut(sums[pl.ds(side, half, stride=2), :]) for side in range(2)))
    for o in range(owners):
        live = jnp.broadcast_to(lives[pl.ds(o, 1), :], high[0].shape) > 0
        for side in range(2):
            for term, piece in enumerate((high, high, low)):
                columns = pl.ds((2 * term + side) * tokens, tokens)
                picked[pl.ds(o * half, half), columns] = jnp.where(
                    live, piece[side], jnp.zeros((), piece[side].dtype)
                )
    grads = lax.dot_general(picked[...], other[...], NT, preferred_element_type=jnp.float32)
    out[...] = grads.reshape(out.shape)


def collect(parts, out):
    seqs, width = out.shape
    lanes = parts.shape[1]
    blocks = width // lanes
    terms = parts.shape[0] // (seqs * blocks)
    for s in range(seqs):
        for c in range(blocks):
            block = parts[pl.ds(s * terms * blocks + c, terms, stride=blocks), :]
            out[pl.ds(s, 1), pl.ds(c * lanes, lanes)] = jnp.sum(block, axis=0, keepdims=True)


def on_device(acts, out_grads, proj_in, proj_out, doc_lengths, owner_map):
    owners = lax.axis_size("dp")
    split = lax.axis_size("tensor")
    length, hidden = acts.shape
    width = out_grads.shape[1]
    rank = proj_in.shape[1]
    lanes = 2 * rank
    depth = math.gcd(512, math.gcd(hidden, width))
    chunks = (hidden + width) // depth
    pairs = split // 2
    tokens = length // split
    half = length // 2
    vmem = pl.BlockSpec(memory_space=pltpu.VMEM)
    smem = pl.BlockSpec(memory_space=pltpu.SMEM)
    hbm = pl.BlockSpec(memory_space=pl.ANY)
    small = pltpu.CompilerParams(vmem_limit_bytes=8 << 20)

    at = lax.axis_index("tensor").astype(jnp.int32).reshape(1)
    sums = pl.pallas_call(
        project,
        out_shape=pltpu.VMEM((length, lanes), jnp.float32),
        in_specs=[hbm] * 4,
        out_specs=vmem,
        scratch_shapes=[
            pltpu.VMEM((chunks, length, depth), acts.dtype),
            pltpu.VMEM((lanes, hidden + width), proj_in.dtype),
            pltpu.SemaphoreType.DMA((2,)),
            pltpu.SemaphoreType.DMA((chunks,)),
        ],
        compiler_params=pltpu.CompilerParams(vmem_limit_bytes=56 << 20),
    )(acts, out_grads, proj_in.T, proj_out.T)
    sent = lax.dynamic_slice_in_dim(sums, (1 - at[0] % 2) * half, half, 0)
    got = lax.ppermute(sent, "tensor", [(i, i ^ 1) for i in range(split)])
    order = tuple(range(1, pairs))
    own, *coded = pl.pallas_call(
        functools.partial(code, order),
        out_shape=(pltpu.VMEM((lanes, tokens), jnp.float32),)
        + (pltpu.VMEM((lanes + 16, tokens), jnp.int16),) * (pairs - 1),
        in_specs=[smem, vmem, vmem],
        out_specs=(vmem,) * pairs,
        compiler_params=small,
    )(at, sums, got)
    parts = [
        lax.ppermute(block, "tensor", [(i, i ^ (2 * m)) for i in range(split)])
        for m, block in zip(order, coded)
    ]
    lives = pl.pallas_call(
        functools.partial(members, pairs),
        out_shape=pltpu.VMEM((owners, tokens), jnp.float32),
        in_specs=[smem] * 3,
        out_specs=vmem,
        compiler_params=small,
    )(doc_lengths, owner_map, at)
    grads = pl.pallas_call(
        outer,
        out_shape=pltpu.VMEM((owners, rank // 2, lanes), jnp.float32),
        in_specs=[vmem] * (pairs + 1),
        out_specs=vmem,
        scratch_shapes=[
            pltpu.VMEM((rank, tokens), jnp.float32),
            pltpu.VMEM((owners * rank // 2, 6 * tokens), jnp.bfloat16),
            pltpu.VMEM((lanes, 6 * tokens), jnp.bfloat16),
        ],
        compiler_params=small,
    )(lives, own, *parts)
    got = lax.all_to_all(
        grads.reshape(owners * rank // 2, lanes), ("dp", "tensor"), 0, 0, tiled=True
    )
    return pl.pallas_call(
        collect,
        out_shape=jax.ShapeDtypeStruct((owners, rank * rank // split), jnp.float32),
        in_specs=[vmem],
        out_specs=vmem,
        compiler_params=small,
    )(got)


def solution(mesh):
    in_specs = (
        P("dp", "tensor"),
        P("dp", "tensor"),
        P("tensor", None),
        P("tensor", None),
        P("dp", None),
        P("dp", None),
    )
    out_specs = P("dp", "tensor")
    return jax.shard_map(
        on_device, mesh=mesh, in_specs=in_specs, out_specs=out_specs, check_vma=False
    )
```

```python
import functools
import math
import jax
import jax.numpy as jnp
from jax import lax
from jax.experimental import pallas as pl
from jax.experimental.pallas import tpu as pltpu
from jax.sharding import PartitionSpec as P

NT = (((1,), (1,)), ((), ()))
TOP = 32767.0


def add_product(out, first, left, right):
    rows = left.shape[0] // 2
    for at in range(0, left.shape[0], rows):
        part = left[pl.ds(at, rows), :]
        term = lax.dot_general(part, right, NT, preferred_element_type=jnp.float32)
        if first:
            out[pl.ds(at, rows), :] = term
        else:
            out[pl.ds(at, rows), :] += term


def columns_of(acts_hbm, grads_hbm, base, half, depth, i, to, sem):
    rows = pl.ds(pl.multiple_of(base, half), half)
    width = grads_hbm.shape[1]
    if i * depth < width:
        source = grads_hbm.at[rows, pl.ds(i * depth, depth)]
    else:
        source = acts_hbm.at[rows, pl.ds(i * depth - width, depth)]
    return pltpu.make_async_copy(source, to, sem)


def project_sent(at, acts_hbm, grads_hbm, in_hbm, out_hbm, sent, weights, early, held, w_sems, sems):
    rank = in_hbm.shape[0]
    chunks, half, depth = held.shape
    hidden, width = acts_hbm.shape[1], grads_hbm.shape[1]
    core = lax.rem(at[0], 2)
    copies = [
        columns_of(acts_hbm, grads_hbm, (1 - core) * half, half, depth, i, held.at[i], sems.at[i])
        for i in range(chunks)
    ] + [
        columns_of(acts_hbm, grads_hbm, core * half, half, depth, i, early.at[i], sems.at[chunks + i])
        for i in range(early.shape[0])
    ]
    loads = (
        pltpu.make_async_copy(
            out_hbm, weights.at[pl.ds(rank, rank), pl.ds(0, width)], w_sems.at[0]
        ),
        pltpu.make_async_copy(
            in_hbm, weights.at[pl.ds(0, rank), pl.ds(width, hidden)], w_sems.at[1]
        ),
    )
    loads[0].start()
    copies[0].start()
    loads[1].start()
    for copy in copies[1:8]:
        copy.start()
    weights[pl.ds(0, rank), pl.ds(0, width)] = jnp.zeros((rank, width), weights.dtype)
    weights[pl.ds(rank, rank), pl.ds(width, hidden)] = jnp.zeros((rank, hidden), weights.dtype)
    loads[0].wait()
    for i in range(chunks):
        if i * depth == width:
            loads[1].wait()
        copies[i].wait()
        if i + 8 < len(copies):
            copies[i + 8].start()
        add_product(sent, i == 0, held.at[i], weights[:, i * depth : (i + 1) * depth])
    for copy in copies[chunks:]:
        copy.wait()


def project_kept(at, acts_hbm, grads_hbm, weights, early, kept, held, sems):
    rest, half, depth = held.shape
    ready = early.shape[0]
    core = lax.rem(at[0], 2)
    copies = [
        columns_of(acts_hbm, grads_hbm, core * half, half, depth, ready + i, held.at[i], sems.at[i])
        for i in range(rest)
    ]
    for copy in copies[:8]:
        copy.start()
    for i in range(ready + rest):
        if i < ready:
            left = early.at[i]
        else:
            left = held.at[i - ready]
            copies[i - ready].wait()
            if i - ready + 8 < rest:
                copies[i - ready + 8].start()
        add_product(kept, i == 0, left, weights[:, i * depth : (i + 1) * depth])


def code(order, at, kept, got, own, *sent):
    lanes, tokens = own.shape
    rank = lanes // 2
    pair = at[0] // 2

    def block(m):
        rows = pl.ds(pl.multiple_of((pair ^ m) * tokens, tokens), tokens)
        return (kept[rows, :] + got[rows, :]).T

    own[...] = block(0)
    for m, out in zip(order, sent):
        value = block(m)
        powers = []
        for side in range(2):
            part = value[side * rank : (side + 1) * rank]
            largest = jnp.max(jnp.abs(part), axis=0, keepdims=True)
            power = jnp.ceil(jnp.log2(jnp.maximum(largest, 1e-30)))
            steps = jnp.round(part * jnp.exp2(15.0 - power))
            steps = jnp.minimum(jnp.maximum(steps, -TOP), TOP).astype(jnp.int32)
            out[pl.ds(side * rank, rank), :] = steps.astype(jnp.int16)
            powers.append(power)
        row = lax.broadcasted_iota(jnp.int32, (out.shape[0] - lanes, tokens), 0)
        power = jnp.where(row == 0, powers[0], powers[1]).astype(jnp.int32)
        out[pl.ds(lanes, row.shape[0]), :] = power.astype(jnp.int16)


def members(pairs, doc_len, doc_owner, at, lives):
    owners, tokens = lives.shape
    docs = doc_len.shape[1]
    core, pair = lax.rem(at[0], 2), at[0] // 2
    first_token = (core * pairs + pair) * tokens
    place = first_token + lax.broadcasted_iota(jnp.int32, (1, tokens), 1)
    starts = []
    start = jnp.int32(0)
    for k in range(docs):
        starts.append(start)
        start = start + doc_len[0, k]
    for o in range(owners):
        first, last = jnp.int32(0), jnp.int32(0)
        for k in range(docs):
            mine = doc_owner[0, k] == o
            first = jnp.where(mine, starts[k], first)
            last = jnp.where(mine, starts[k] + doc_len[0, k], last)
        lives[pl.ds(o, 1), :] = ((place >= first) & (place < last)).astype(jnp.float32)


def cut(value):
    high = value.astype(jnp.bfloat16)
    return high, (value - high.astype(jnp.float32)).astype(jnp.bfloat16)


def outer(lives, own, *refs):
    *parts, out, sums, picked, other = refs
    lanes, tokens = own.shape
    owners = out.shape[0]
    rank = lanes // 2
    half = rank // 2
    sides = [own[pl.ds(0, rank), :], own[pl.ds(rank, rank), :]]
    for part in parts:
        powers = part[pl.ds(lanes, part.shape[0] - lanes), :].astype(jnp.int32)
        scales = jnp.exp2(powers.astype(jnp.float32) - 15.0)
        for side in range(2):
            steps = part[pl.ds(side * rank, rank), :].astype(jnp.int32).astype(jnp.float32)
            sides[side] = sides[side] + steps * scales[side : side + 1]
    sums[...] = sides[1]
    high, low = cut(sides[0])
    other[...] = jnp.zeros(other.shape, other.dtype)
    for side in range(2):
        for term, piece in enumerate((high, low, high)):
            columns = pl.ds((2 * term + side) * tokens, tokens)
            other[pl.ds(side * rank, rank), columns] = piece
    high, low = zip(*(cut(sums[pl.ds(side, half, stride=2), :]) for side in range(2)))
    for o in range(owners):
        live = jnp.broadcast_to(lives[pl.ds(o, 1), :], high[0].shape) > 0
        for side in range(2):
            for term, piece in enumerate((high, high, low)):
                columns = pl.ds((2 * term + side) * tokens, tokens)
                picked[pl.ds(o * half, half), columns] = jnp.where(
                    live, piece[side], jnp.zeros((), piece[side].dtype)
                )
    grads = lax.dot_general(picked[...], other[...], NT, preferred_element_type=jnp.float32)
    out[...] = grads.reshape(out.shape)


def on_device(acts, out_grads, proj_in, proj_out, doc_lengths, owner_map):
    owners = lax.axis_size("dp")
    split = lax.axis_size("tensor")
    length, hidden = acts.shape
    width = out_grads.shape[1]
    rank = proj_in.shape[1]
    lanes = 2 * rank
    depth = math.gcd(512, math.gcd(hidden, width))
    chunks = (hidden + width) // depth
    pairs = split // 2
    tokens = length // split
    half = length // 2
    vmem = pl.BlockSpec(memory_space=pltpu.VMEM)
    smem = pl.BlockSpec(memory_space=pltpu.SMEM)
    hbm = pl.BlockSpec(memory_space=pl.ANY)
    small = pltpu.CompilerParams(vmem_limit_bytes=8 << 20)

    at = lax.axis_index("tensor").astype(jnp.int32).reshape(1)
    acts, out_grads, w_in, w_out = (
        pltpu.with_memory_space_constraint(array, pltpu.HBM)
        for array in (acts, out_grads, proj_in.T, proj_out.T)
    )
    ready = min(3, chunks - 1)
    sums = pltpu.VMEM((half, lanes), jnp.float32)
    medium = pltpu.CompilerParams(vmem_limit_bytes=16 << 20)
    cost = pl.CostEstimate(
        flops=2 * half * lanes * (hidden + width),
        bytes_accessed=2 * half * (hidden + width),
        transcendentals=0,
    )
    sent, weights, early = pl.pallas_call(
        project_sent,
        out_shape=(
            sums,
            pltpu.VMEM((lanes, hidden + width), proj_in.dtype),
            pltpu.VMEM((ready, half, depth), acts.dtype),
        ),
        in_specs=[smem] + [hbm] * 4,
        out_specs=(vmem,) * 3,
        scratch_shapes=[
            pltpu.VMEM((chunks, half, depth), acts.dtype),
            pltpu.SemaphoreType.DMA((2,)),
            pltpu.SemaphoreType.DMA((chunks + ready,)),
        ],
        compiler_params=medium,
        cost_estimate=cost,
    )(at, acts, out_grads, w_in, w_out)
    got = lax.ppermute(sent, "tensor", [(i, i ^ 1) for i in range(split)])
    kept = pl.pallas_call(
        project_kept,
        out_shape=sums,
        in_specs=[smem, hbm, hbm, vmem, vmem],
        out_specs=vmem,
        scratch_shapes=[
            pltpu.VMEM((chunks - ready, half, depth), acts.dtype),
            pltpu.SemaphoreType.DMA((chunks - ready,)),
        ],
        compiler_params=medium,
        cost_estimate=cost,
    )(at, acts, out_grads, weights, early)
    order = tuple(range(1, pairs))
    own, *coded = pl.pallas_call(
        functools.partial(code, order),
        out_shape=(pltpu.VMEM((lanes, tokens), jnp.float32),)
        + (pltpu.VMEM((lanes + 16, tokens), jnp.int16),) * (pairs - 1),
        in_specs=[smem, vmem, vmem],
        out_specs=(vmem,) * pairs,
        compiler_params=small,
    )(at, kept, got)
    parts = [
        lax.ppermute(block, "tensor", [(i, i ^ (2 * m)) for i in range(split)])
        for m, block in zip(order, coded)
    ]
    lives = pl.pallas_call(
        functools.partial(members, pairs),
        out_shape=pltpu.VMEM((owners, tokens), jnp.float32),
        in_specs=[smem] * 3,
        out_specs=vmem,
        compiler_params=small,
    )(doc_lengths, owner_map, at)
    grads = pl.pallas_call(
        outer,
        out_shape=pltpu.VMEM((owners, rank // 2, lanes), jnp.float32),
        in_specs=[vmem] * (pairs + 1),
        out_specs=vmem,
        scratch_shapes=[
            pltpu.VMEM((rank, tokens), jnp.float32),
            pltpu.VMEM((owners * rank // 2, 6 * tokens), jnp.bfloat16),
            pltpu.VMEM((lanes, 6 * tokens), jnp.bfloat16),
        ],
        compiler_params=small,
    )(lives, own, *parts)
    got = lax.all_to_all(
        grads.reshape(owners * rank // 2, lanes), ("dp", "tensor"), 0, 0, tiled=True
    )
    blocks = rank * rank // (split * lanes)
    return jnp.sum(got.reshape(owners, split, blocks, lanes), 1).reshape(owners, blocks * lanes)


def solution(mesh):
    in_specs = (
        P("dp", "tensor"),
        P("dp", "tensor"),
        P("tensor", None),
        P("tensor", None),
        P("dp", None),
        P("dp", None),
    )
    out_specs = P("dp", "tensor")
    return jax.shard_map(
        on_device, mesh=mesh, in_specs=in_specs, out_specs=out_specs, check_vma=False
    )
```

```python
import functools
import math
import jax
import jax.numpy as jnp
from jax import lax
from jax.experimental import pallas as pl
from jax.experimental.pallas import tpu as pltpu
from jax.sharding import PartitionSpec as P

NT = (((1,), (1,)), ((), ()))
TOP = 32767.0


def project(acts_hbm, grads_hbm, in_hbm, out_hbm, sums, held, weights, w_sems, sems):
    rank = in_hbm.shape[0]
    chunks, length, depth = held.shape
    hidden, width = acts_hbm.shape[1], grads_hbm.shape[1]
    rows = length // 4
    ahead = min(5, chunks)

    def copy(i):
        if i * depth < width:
            source = grads_hbm.at[:, pl.ds(i * depth, depth)]
        else:
            source = acts_hbm.at[:, pl.ds(i * depth - width, depth)]
        return pltpu.make_async_copy(source, held.at[i], sems.at[i])

    loads = (
        pltpu.make_async_copy(
            out_hbm, weights.at[pl.ds(rank, rank), pl.ds(0, width)], w_sems.at[0]
        ),
        pltpu.make_async_copy(
            in_hbm, weights.at[pl.ds(0, rank), pl.ds(width, hidden)], w_sems.at[1]
        ),
    )
    loads[0].start()
    copy(0).start()
    loads[1].start()
    for i in range(1, ahead):
        copy(i).start()
    weights[pl.ds(0, rank), pl.ds(0, width)] = jnp.zeros((rank, width), weights.dtype)
    weights[pl.ds(rank, rank), pl.ds(width, hidden)] = jnp.zeros((rank, hidden), weights.dtype)
    loads[0].wait()
    for i in range(chunks):
        if i * depth == width:
            loads[1].wait()
        copy(i).wait()
        if i + ahead < chunks:
            copy(i + ahead).start()
        block = weights[:, i * depth : (i + 1) * depth]
        for at in range(0, length, rows):
            part = held[i, pl.ds(at, rows), :]
            term = lax.dot_general(part, block, NT, preferred_element_type=jnp.float32)
            if i:
                sums[pl.ds(at, rows), :] += term
            else:
                sums[pl.ds(at, rows), :] = term


def code(order, at, sums, got, own, *sent):
    lanes, tokens = own.shape
    rank = lanes // 2
    pair = at[0] // 2
    kept = lax.rem(at[0], 2) * got.shape[0]

    def block(m):
        start = pl.multiple_of((pair ^ m) * tokens, tokens)
        mine = pl.ds(pl.multiple_of(kept + start, tokens), tokens)
        return (sums[mine, :] + got[pl.ds(start, tokens), :]).T

    own[...] = block(0)
    for m, out in zip(order, sent):
        value = block(m)
        powers = []
        for side in range(2):
            part = value[side * rank : (side + 1) * rank]
            largest = jnp.max(jnp.abs(part), axis=0, keepdims=True)
            power = jnp.ceil(jnp.log2(jnp.maximum(largest, 1e-30)))
            steps = jnp.round(part * jnp.exp2(15.0 - power))
            steps = jnp.minimum(jnp.maximum(steps, -TOP), TOP).astype(jnp.int32)
            out[pl.ds(side * rank, rank), :] = steps.astype(jnp.int16)
            powers.append(power)
        row = lax.broadcasted_iota(jnp.int32, (out.shape[0] - lanes, tokens), 0)
        power = jnp.where(row == 0, powers[0], powers[1]).astype(jnp.int32)
        out[pl.ds(lanes, row.shape[0]), :] = power.astype(jnp.int16)


def members(pairs, doc_len, doc_owner, at, lives):
    owners, tokens = lives.shape
    docs = doc_len.shape[1]
    core, pair = lax.rem(at[0], 2), at[0] // 2
    first_token = (core * pairs + pair) * tokens
    place = first_token + lax.broadcasted_iota(jnp.int32, (1, tokens), 1)
    starts = []
    start = jnp.int32(0)
    for k in range(docs):
        starts.append(start)
        start = start + doc_len[0, k]
    for o in range(owners):
        first, last = jnp.int32(0), jnp.int32(0)
        for k in range(docs):
            mine = doc_owner[0, k] == o
            first = jnp.where(mine, starts[k], first)
            last = jnp.where(mine, starts[k] + doc_len[0, k], last)
        lives[pl.ds(o, 1), :] = ((place >= first) & (place < last)).astype(jnp.float32)


def cut(value):
    high = value.astype(jnp.bfloat16)
    return high, (value - high.astype(jnp.float32)).astype(jnp.bfloat16)


def outer(lives, own, *refs):
    *parts, out, sums, picked, other = refs
    lanes, tokens = own.shape
    owners = out.shape[0]
    rank = lanes // 2
    half = rank // 2
    sides = [own[pl.ds(0, rank), :], own[pl.ds(rank, rank), :]]
    for part in parts:
        powers = part[pl.ds(lanes, part.shape[0] - lanes), :].astype(jnp.int32)
        scales = jnp.exp2(powers.astype(jnp.float32) - 15.0)
        for side in range(2):
            steps = part[pl.ds(side * rank, rank), :].astype(jnp.int32).astype(jnp.float32)
            sides[side] = sides[side] + steps * scales[side : side + 1]
    sums[...] = sides[1]
    high, low = cut(sides[0])
    other[...] = jnp.zeros(other.shape, other.dtype)
    for side in range(2):
        for term, piece in enumerate((high, low, high)):
            columns = pl.ds((2 * term + side) * tokens, tokens)
            other[pl.ds(side * rank, rank), columns] = piece
    high, low = zip(*(cut(sums[pl.ds(side, half, stride=2), :]) for side in range(2)))
    for o in range(owners):
        live = jnp.broadcast_to(lives[pl.ds(o, 1), :], high[0].shape) > 0
        for side in range(2):
            for term, piece in enumerate((high, high, low)):
                columns = pl.ds((2 * term + side) * tokens, tokens)
                picked[pl.ds(o * half, half), columns] = jnp.where(
                    live, piece[side], jnp.zeros((), piece[side].dtype)
                )
    grads = lax.dot_general(picked[...], other[...], NT, preferred_element_type=jnp.float32)
    out[...] = grads.reshape(out.shape)


def on_device(acts, out_grads, proj_in, proj_out, doc_lengths, owner_map):
    owners = lax.axis_size("dp")
    split = lax.axis_size("tensor")
    length, hidden = acts.shape
    width = out_grads.shape[1]
    rank = proj_in.shape[1]
    lanes = 2 * rank
    depth = math.gcd(512, math.gcd(hidden, width))
    chunks = (hidden + width) // depth
    pairs = split // 2
    tokens = length // split
    half = length // 2
    vmem = pl.BlockSpec(memory_space=pltpu.VMEM)
    smem = pl.BlockSpec(memory_space=pltpu.SMEM)
    hbm = pl.BlockSpec(memory_space=pl.ANY)
    small = pltpu.CompilerParams(vmem_limit_bytes=8 << 20)

    at = lax.axis_index("tensor").astype(jnp.int32).reshape(1)
    sums = pl.pallas_call(
        project,
        out_shape=pltpu.VMEM((length, lanes), jnp.float32),
        in_specs=[hbm] * 4,
        out_specs=vmem,
        scratch_shapes=[
            pltpu.VMEM((chunks, length, depth), acts.dtype),
            pltpu.VMEM((lanes, hidden + width), proj_in.dtype),
            pltpu.SemaphoreType.DMA((2,)),
            pltpu.SemaphoreType.DMA((chunks,)),
        ],
        compiler_params=pltpu.CompilerParams(vmem_limit_bytes=56 << 20),
    )(acts, out_grads, proj_in.T, proj_out.T)
    sent = lax.dynamic_slice_in_dim(sums, (1 - at[0] % 2) * half, half, 0)
    got = lax.ppermute(sent, "tensor", [(i, i ^ 1) for i in range(split)])
    order = tuple(range(1, pairs))
    own, *coded = pl.pallas_call(
        functools.partial(code, order),
        out_shape=(pltpu.VMEM((lanes, tokens), jnp.float32),)
        + (pltpu.VMEM((lanes + 16, tokens), jnp.int16),) * (pairs - 1),
        in_specs=[smem, vmem, vmem],
        out_specs=(vmem,) * pairs,
        compiler_params=small,
    )(at, sums, got)
    parts = [
        lax.ppermute(block, "tensor", [(i, i ^ (2 * m)) for i in range(split)])
        for m, block in zip(order, coded)
    ]
    lives = pl.pallas_call(
        functools.partial(members, pairs),
        out_shape=pltpu.VMEM((owners, tokens), jnp.float32),
        in_specs=[smem] * 3,
        out_specs=vmem,
        compiler_params=small,
    )(doc_lengths, owner_map, at)
    grads = pl.pallas_call(
        outer,
        out_shape=pltpu.VMEM((owners, rank // 2, lanes), jnp.float32),
        in_specs=[vmem] * (pairs + 1),
        out_specs=vmem,
        scratch_shapes=[
            pltpu.VMEM((rank, tokens), jnp.float32),
            pltpu.VMEM((owners * rank // 2, 6 * tokens), jnp.bfloat16),
            pltpu.VMEM((lanes, 6 * tokens), jnp.bfloat16),
        ],
        compiler_params=small,
    )(lives, own, *parts)
    got = lax.all_to_all(
        grads.reshape(owners * rank // 2, lanes), ("dp", "tensor"), 0, 0, tiled=True
    )
    blocks = rank * rank // (split * lanes)
    return jnp.sum(got.reshape(owners, split, blocks, lanes), 1).reshape(owners, blocks * lanes)


def solution(mesh):
    in_specs = (
        P("dp", "tensor"),
        P("dp", "tensor"),
        P("tensor", None),
        P("tensor", None),
        P("dp", None),
        P("dp", None),
    )
    out_specs = P("dp", "tensor")
    return jax.shard_map(
        on_device, mesh=mesh, in_specs=in_specs, out_specs=out_specs, check_vma=False
    )
```

```python
import functools
import math
import jax
import jax.numpy as jnp
from jax import lax
from jax.experimental import pallas as pl
from jax.experimental.pallas import tpu as pltpu
from jax.sharding import PartitionSpec as P

NT = (((1,), (1,)), ((), ()))
TOP = 32767.0


def add_product(out, first, left, right):
    rows = left.shape[0] // 2
    for at in range(0, left.shape[0], rows):
        part = left[pl.ds(at, rows), :]
        term = lax.dot_general(part, right, NT, preferred_element_type=jnp.float32)
        if first:
            out[pl.ds(at, rows), :] = term
        else:
            out[pl.ds(at, rows), :] += term


def columns_of(acts_hbm, grads_hbm, base, half, depth, i, to, sem):
    rows = pl.ds(pl.multiple_of(base, half), half)
    width = grads_hbm.shape[1]
    if i * depth < width:
        source = grads_hbm.at[rows, pl.ds(i * depth, depth)]
    else:
        source = acts_hbm.at[rows, pl.ds(i * depth - width, depth)]
    return pltpu.make_async_copy(source, to, sem)


def project_sent(at, acts_hbm, grads_hbm, in_hbm, out_hbm, sent, weights, early, held, w_sems, sems):
    rank = in_hbm.shape[0]
    chunks, half, depth = held.shape
    hidden, width = acts_hbm.shape[1], grads_hbm.shape[1]
    core = lax.rem(at[0], 2)
    copies = [
        columns_of(acts_hbm, grads_hbm, (1 - core) * half, half, depth, i, held.at[i], sems.at[i])
        for i in range(chunks)
    ] + [
        columns_of(acts_hbm, grads_hbm, core * half, half, depth, i, early.at[i], sems.at[chunks + i])
        for i in range(early.shape[0])
    ]
    loads = (
        pltpu.make_async_copy(
            out_hbm, weights.at[pl.ds(rank, rank), pl.ds(0, width)], w_sems.at[0]
        ),
        pltpu.make_async_copy(
            in_hbm, weights.at[pl.ds(0, rank), pl.ds(width, hidden)], w_sems.at[1]
        ),
    )
    loads[0].start()
    copies[0].start()
    loads[1].start()
    for copy in copies[1:8]:
        copy.start()
    weights[pl.ds(0, rank), pl.ds(0, width)] = jnp.zeros((rank, width), weights.dtype)
    weights[pl.ds(rank, rank), pl.ds(width, hidden)] = jnp.zeros((rank, hidden), weights.dtype)
    loads[0].wait()
    for i in range(chunks):
        if i * depth == width:
            loads[1].wait()
        copies[i].wait()
        if i + 8 < len(copies):
            copies[i + 8].start()
        add_product(sent, i == 0, held.at[i], weights[:, i * depth : (i + 1) * depth])
    for copy in copies[chunks:]:
        copy.wait()


def project_kept(at, acts_hbm, grads_hbm, weights, early, kept, held, sems):
    rest, half, depth = held.shape
    ready = early.shape[0]
    core = lax.rem(at[0], 2)
    copies = [
        columns_of(acts_hbm, grads_hbm, core * half, half, depth, ready + i, held.at[i], sems.at[i])
        for i in range(rest)
    ]
    for copy in copies[:8]:
        copy.start()
    for i in range(ready + rest):
        if i < ready:
            left = early.at[i]
        else:
            left = held.at[i - ready]
            copies[i - ready].wait()
            if i - ready + 8 < rest:
                copies[i - ready + 8].start()
        add_product(kept, i == 0, left, weights[:, i * depth : (i + 1) * depth])


def code(order, at, kept, got, own, *sent):
    lanes, tokens = own.shape
    rank = lanes // 2
    pair = at[0] // 2

    def block(m):
        rows = pl.ds(pl.multiple_of((pair ^ m) * tokens, tokens), tokens)
        return (kept[rows, :] + got[rows, :]).T

    own[...] = block(0)
    for m, out in zip(order, sent):
        value = block(m)
        powers = []
        for side in range(2):
            part = value[side * rank : (side + 1) * rank]
            largest = jnp.max(jnp.abs(part), axis=0, keepdims=True)
            power = jnp.ceil(jnp.log2(jnp.maximum(largest, 1e-30)))
            steps = jnp.round(part * jnp.exp2(15.0 - power))
            steps = jnp.minimum(jnp.maximum(steps, -TOP), TOP).astype(jnp.int32)
            out[pl.ds(side * rank, rank), :] = steps.astype(jnp.int16)
            powers.append(power)
        row = lax.broadcasted_iota(jnp.int32, (out.shape[0] - lanes, tokens), 0)
        power = jnp.where(row == 0, powers[0], powers[1]).astype(jnp.int32)
        out[pl.ds(lanes, row.shape[0]), :] = power.astype(jnp.int16)


def members(pairs, doc_len, doc_owner, at, lives):
    owners, tokens = lives.shape
    docs = doc_len.shape[1]
    core, pair = lax.rem(at[0], 2), at[0] // 2
    first_token = (core * pairs + pair) * tokens
    place = first_token + lax.broadcasted_iota(jnp.int32, (1, tokens), 1)
    starts = []
    start = jnp.int32(0)
    for k in range(docs):
        starts.append(start)
        start = start + doc_len[0, k]
    for o in range(owners):
        first, last = jnp.int32(0), jnp.int32(0)
        for k in range(docs):
            mine = doc_owner[0, k] == o
            first = jnp.where(mine, starts[k], first)
            last = jnp.where(mine, starts[k] + doc_len[0, k], last)
        lives[pl.ds(o, 1), :] = ((place >= first) & (place < last)).astype(jnp.float32)


def cut(value):
    high = value.astype(jnp.bfloat16)
    return high, (value - high.astype(jnp.float32)).astype(jnp.bfloat16)


def outer(lives, own, *refs):
    *parts, out, sums, picked, other = refs
    lanes, tokens = own.shape
    owners = out.shape[0]
    rank = lanes // 2
    half = rank // 2
    sides = [own[pl.ds(0, rank), :], own[pl.ds(rank, rank), :]]
    for part in parts:
        powers = part[pl.ds(lanes, part.shape[0] - lanes), :].astype(jnp.int32)
        scales = jnp.exp2(powers.astype(jnp.float32) - 15.0)
        for side in range(2):
            steps = part[pl.ds(side * rank, rank), :].astype(jnp.int32).astype(jnp.float32)
            sides[side] = sides[side] + steps * scales[side : side + 1]
    sums[...] = sides[1]
    high, low = cut(sides[0])
    other[...] = jnp.zeros(other.shape, other.dtype)
    for side in range(2):
        for term, piece in enumerate((high, low, high)):
            columns = pl.ds((2 * term + side) * tokens, tokens)
            other[pl.ds(side * rank, rank), columns] = piece
    high, low = zip(*(cut(sums[pl.ds(side, half, stride=2), :]) for side in range(2)))
    for o in range(owners):
        live = jnp.broadcast_to(lives[pl.ds(o, 1), :], high[0].shape) > 0
        for side in range(2):
            for term, piece in enumerate((high, high, low)):
                columns = pl.ds((2 * term + side) * tokens, tokens)
                picked[pl.ds(o * half, half), columns] = jnp.where(
                    live, piece[side], jnp.zeros((), piece[side].dtype)
                )
    grads = lax.dot_general(picked[...], other[...], NT, preferred_element_type=jnp.float32)
    out[...] = grads.reshape(out.shape)


def on_device(acts, out_grads, proj_in, proj_out, doc_lengths, owner_map):
    owners = lax.axis_size("dp")
    split = lax.axis_size("tensor")
    length, hidden = acts.shape
    width = out_grads.shape[1]
    rank = proj_in.shape[1]
    lanes = 2 * rank
    depth = math.gcd(512, math.gcd(hidden, width))
    chunks = (hidden + width) // depth
    pairs = split // 2
    tokens = length // split
    half = length // 2
    vmem = pl.BlockSpec(memory_space=pltpu.VMEM)
    smem = pl.BlockSpec(memory_space=pltpu.SMEM)
    hbm = pl.BlockSpec(memory_space=pl.ANY)
    small = pltpu.CompilerParams(vmem_limit_bytes=8 << 20)

    at = lax.axis_index("tensor").astype(jnp.int32).reshape(1)
    acts, out_grads, w_in, w_out = (
        pltpu.with_memory_space_constraint(array, pltpu.HBM)
        for array in (acts, out_grads, proj_in.T, proj_out.T)
    )
    ready = min(3, chunks - 1)
    sums = pltpu.VMEM((half, lanes), jnp.float32)
    medium = pltpu.CompilerParams(vmem_limit_bytes=16 << 20)
    cost = pl.CostEstimate(
        flops=2 * half * lanes * (hidden + width),
        bytes_accessed=2 * half * (hidden + width),
        transcendentals=0,
    )
    sent, weights, early = pl.pallas_call(
        project_sent,
        out_shape=(
            sums,
            pltpu.VMEM((lanes, hidden + width), proj_in.dtype),
            pltpu.VMEM((ready, half, depth), acts.dtype),
        ),
        in_specs=[smem] + [hbm] * 4,
        out_specs=(vmem,) * 3,
        scratch_shapes=[
            pltpu.VMEM((chunks, half, depth), acts.dtype),
            pltpu.SemaphoreType.DMA((2,)),
            pltpu.SemaphoreType.DMA((chunks + ready,)),
        ],
        compiler_params=medium,
        cost_estimate=cost,
    )(at, acts, out_grads, w_in, w_out)
    got = lax.ppermute(sent, "tensor", [(i, i ^ 1) for i in range(split)])
    kept = pl.pallas_call(
        project_kept,
        out_shape=sums,
        in_specs=[smem, hbm, hbm, vmem, vmem],
        out_specs=vmem,
        scratch_shapes=[
            pltpu.VMEM((chunks - ready, half, depth), acts.dtype),
            pltpu.SemaphoreType.DMA((chunks - ready,)),
        ],
        compiler_params=medium,
        cost_estimate=cost,
    )(at, acts, out_grads, weights, early)
    order = tuple(range(pairs - 1, 0, -1))
    own, *coded = pl.pallas_call(
        functools.partial(code, order),
        out_shape=(pltpu.VMEM((lanes, tokens), jnp.float32),)
        + (pltpu.VMEM((lanes + 16, tokens), jnp.int16),) * (pairs - 1),
        in_specs=[smem, vmem, vmem],
        out_specs=(vmem,) * pairs,
        compiler_params=small,
    )(at, kept, got)
    parts = [
        lax.ppermute(block, "tensor", [(i, i ^ (2 * m)) for i in range(split)])
        for m, block in zip(order, coded)
    ]
    lives = pl.pallas_call(
        functools.partial(members, pairs),
        out_shape=pltpu.VMEM((owners, tokens), jnp.float32),
        in_specs=[smem] * 3,
        out_specs=vmem,
        compiler_params=small,
    )(doc_lengths, owner_map, at)
    grads = pl.pallas_call(
        outer,
        out_shape=pltpu.VMEM((owners, rank // 2, lanes), jnp.float32),
        in_specs=[vmem] * (pairs + 1),
        out_specs=vmem,
        scratch_shapes=[
            pltpu.VMEM((rank, tokens), jnp.float32),
            pltpu.VMEM((owners * rank // 2, 6 * tokens), jnp.bfloat16),
            pltpu.VMEM((lanes, 6 * tokens), jnp.bfloat16),
        ],
        compiler_params=small,
    )(lives, own, *parts)
    got = lax.all_to_all(
        grads.reshape(owners * rank // 2, lanes), ("dp", "tensor"), 0, 0, tiled=True
    )
    blocks = rank * rank // (split * lanes)
    return jnp.sum(got.reshape(owners, split, blocks, lanes), 1).reshape(owners, blocks * lanes)


def solution(mesh):
    in_specs = (
        P("dp", "tensor"),
        P("dp", "tensor"),
        P("tensor", None),
        P("tensor", None),
        P("dp", None),
        P("dp", None),
    )
    out_specs = P("dp", "tensor")
    return jax.shard_map(
        on_device, mesh=mesh, in_specs=in_specs, out_specs=out_specs, check_vma=False
    )
```

```python
import functools
import math
import jax
import jax.numpy as jnp
from jax import lax
from jax.experimental import pallas as pl
from jax.experimental.pallas import tpu as pltpu
from jax.sharding import PartitionSpec as P

NT = (((1,), (1,)), ((), ()))
TOP = 32767.0


def add_product(out, first, left, right):
    rows = left.shape[0] // 2
    for at in range(0, left.shape[0], rows):
        part = left[pl.ds(at, rows), :]
        term = lax.dot_general(part, right, NT, preferred_element_type=jnp.float32)
        if first:
            out[pl.ds(at, rows), :] = term
        else:
            out[pl.ds(at, rows), :] += term


def columns_of(acts_hbm, grads_hbm, base, half, depth, i, to, sem):
    rows = pl.ds(pl.multiple_of(base, half), half)
    width = grads_hbm.shape[1]
    if i * depth < width:
        source = grads_hbm.at[rows, pl.ds(i * depth, depth)]
    else:
        source = acts_hbm.at[rows, pl.ds(i * depth - width, depth)]
    return pltpu.make_async_copy(source, to, sem)


def project_sent(at, acts_hbm, grads_hbm, in_hbm, out_hbm, sent, weights, early, held, w_sems, sems):
    rank = in_hbm.shape[0]
    chunks, half, depth = held.shape
    hidden, width = acts_hbm.shape[1], grads_hbm.shape[1]
    core = lax.rem(at[0], 2)
    copies = [
        columns_of(acts_hbm, grads_hbm, (1 - core) * half, half, depth, i, held.at[i], sems.at[i])
        for i in range(chunks)
    ] + [
        columns_of(acts_hbm, grads_hbm, core * half, half, depth, i, early.at[i], sems.at[chunks + i])
        for i in range(early.shape[0])
    ]
    loads = (
        pltpu.make_async_copy(
            out_hbm, weights.at[pl.ds(rank, rank), pl.ds(0, width)], w_sems.at[0]
        ),
        pltpu.make_async_copy(
            in_hbm, weights.at[pl.ds(0, rank), pl.ds(width, hidden)], w_sems.at[1]
        ),
    )
    loads[0].start()
    copies[0].start()
    loads[1].start()
    for copy in copies[1:6]:
        copy.start()
    weights[pl.ds(0, rank), pl.ds(0, width)] = jnp.zeros((rank, width), weights.dtype)
    weights[pl.ds(rank, rank), pl.ds(width, hidden)] = jnp.zeros((rank, hidden), weights.dtype)
    loads[0].wait()
    for i in range(chunks):
        if i * depth == width:
            loads[1].wait()
        copies[i].wait()
        if i + 6 < len(copies):
            copies[i + 6].start()
        add_product(sent, i == 0, held.at[i], weights[:, i * depth : (i + 1) * depth])
    for copy in copies[chunks:]:
        copy.wait()


def project_kept(at, acts_hbm, grads_hbm, weights, early, kept, held, sems):
    rest, half, depth = held.shape
    ready = early.shape[0]
    core = lax.rem(at[0], 2)
    copies = [
        columns_of(acts_hbm, grads_hbm, core * half, half, depth, ready + i, held.at[i], sems.at[i])
        for i in range(rest)
    ]
    for copy in copies[:6]:
        copy.start()
    for i in range(ready + rest):
        if i < ready:
            left = early.at[i]
        else:
            left = held.at[i - ready]
            copies[i - ready].wait()
            if i - ready + 6 < rest:
                copies[i - ready + 6].start()
        add_product(kept, i == 0, left, weights[:, i * depth : (i + 1) * depth])


def code(order, at, kept, got, own, *sent):
    lanes, tokens = own.shape
    rank = lanes // 2
    pair = at[0] // 2

    def block(m):
        rows = pl.ds(pl.multiple_of((pair ^ m) * tokens, tokens), tokens)
        return (kept[rows, :] + got[rows, :]).T

    own[...] = block(0)
    for m, out in zip(order, sent):
        value = block(m)
        powers = []
        for side in range(2):
            part = value[side * rank : (side + 1) * rank]
            largest = jnp.max(jnp.abs(part), axis=0, keepdims=True)
            power = jnp.ceil(jnp.log2(jnp.maximum(largest, 1e-30)))
            steps = jnp.round(part * jnp.exp2(15.0 - power))
            steps = jnp.minimum(jnp.maximum(steps, -TOP), TOP).astype(jnp.int32)
            out[pl.ds(side * rank, rank), :] = steps.astype(jnp.int16)
            powers.append(power)
        row = lax.broadcasted_iota(jnp.int32, (out.shape[0] - lanes, tokens), 0)
        power = jnp.where(row == 0, powers[0], powers[1]).astype(jnp.int32)
        out[pl.ds(lanes, row.shape[0]), :] = power.astype(jnp.int16)


def members(pairs, doc_len, doc_owner, at, lives):
    owners, tokens = lives.shape
    docs = doc_len.shape[1]
    core, pair = lax.rem(at[0], 2), at[0] // 2
    first_token = (core * pairs + pair) * tokens
    place = first_token + lax.broadcasted_iota(jnp.int32, (1, tokens), 1)
    starts = []
    start = jnp.int32(0)
    for k in range(docs):
        starts.append(start)
        start = start + doc_len[0, k]
    for o in range(owners):
        first, last = jnp.int32(0), jnp.int32(0)
        for k in range(docs):
            mine = doc_owner[0, k] == o
            first = jnp.where(mine, starts[k], first)
            last = jnp.where(mine, starts[k] + doc_len[0, k], last)
        lives[pl.ds(o, 1), :] = ((place >= first) & (place < last)).astype(jnp.float32)


def cut(value):
    high = value.astype(jnp.bfloat16)
    return high, (value - high.astype(jnp.float32)).astype(jnp.bfloat16)


def outer(lives, own, *refs):
    *parts, out, sums, picked, other = refs
    lanes, tokens = own.shape
    owners = out.shape[0]
    rank = lanes // 2
    half = rank // 2
    sides = [own[pl.ds(0, rank), :], own[pl.ds(rank, rank), :]]
    for part in parts:
        powers = part[pl.ds(lanes, part.shape[0] - lanes), :].astype(jnp.int32)
        scales = jnp.exp2(powers.astype(jnp.float32) - 15.0)
        for side in range(2):
            steps = part[pl.ds(side * rank, rank), :].astype(jnp.int32).astype(jnp.float32)
            sides[side] = sides[side] + steps * scales[side : side + 1]
    sums[...] = sides[1]
    high, low = cut(sides[0])
    other[...] = jnp.zeros(other.shape, other.dtype)
    for side in range(2):
        for term, piece in enumerate((high, low, high)):
            columns = pl.ds((2 * term + side) * tokens, tokens)
            other[pl.ds(side * rank, rank), columns] = piece
    high, low = zip(*(cut(sums[pl.ds(side, half, stride=2), :]) for side in range(2)))
    for o in range(owners):
        live = jnp.broadcast_to(lives[pl.ds(o, 1), :], high[0].shape) > 0
        for side in range(2):
            for term, piece in enumerate((high, high, low)):
                columns = pl.ds((2 * term + side) * tokens, tokens)
                picked[pl.ds(o * half, half), columns] = jnp.where(
                    live, piece[side], jnp.zeros((), piece[side].dtype)
                )
    grads = lax.dot_general(picked[...], other[...], NT, preferred_element_type=jnp.float32)
    out[...] = grads.reshape(out.shape)


def on_device(acts, out_grads, proj_in, proj_out, doc_lengths, owner_map):
    owners = lax.axis_size("dp")
    split = lax.axis_size("tensor")
    length, hidden = acts.shape
    width = out_grads.shape[1]
    rank = proj_in.shape[1]
    lanes = 2 * rank
    depth = math.gcd(512, math.gcd(hidden, width))
    chunks = (hidden + width) // depth
    pairs = split // 2
    tokens = length // split
    half = length // 2
    vmem = pl.BlockSpec(memory_space=pltpu.VMEM)
    smem = pl.BlockSpec(memory_space=pltpu.SMEM)
    hbm = pl.BlockSpec(memory_space=pl.ANY)
    small = pltpu.CompilerParams(vmem_limit_bytes=8 << 20)

    at = lax.axis_index("tensor").astype(jnp.int32).reshape(1)
    acts, out_grads, w_in, w_out = (
        pltpu.with_memory_space_constraint(array, pltpu.HBM)
        for array in (acts, out_grads, proj_in.T, proj_out.T)
    )
    ready = min(3, chunks - 1)
    sums = pltpu.VMEM((half, lanes), jnp.float32)
    medium = pltpu.CompilerParams(vmem_limit_bytes=16 << 20)
    cost = pl.CostEstimate(
        flops=2 * half * lanes * (hidden + width),
        bytes_accessed=2 * half * (hidden + width),
        transcendentals=0,
    )
    sent, weights, early = pl.pallas_call(
        project_sent,
        out_shape=(
            sums,
            pltpu.VMEM((lanes, hidden + width), proj_in.dtype),
            pltpu.VMEM((ready, half, depth), acts.dtype),
        ),
        in_specs=[smem] + [hbm] * 4,
        out_specs=(vmem,) * 3,
        scratch_shapes=[
            pltpu.VMEM((chunks, half, depth), acts.dtype),
            pltpu.SemaphoreType.DMA((2,)),
            pltpu.SemaphoreType.DMA((chunks + ready,)),
        ],
        compiler_params=medium,
        cost_estimate=cost,
    )(at, acts, out_grads, w_in, w_out)
    got = lax.ppermute(sent, "tensor", [(i, i ^ 1) for i in range(split)])
    kept = pl.pallas_call(
        project_kept,
        out_shape=sums,
        in_specs=[smem, hbm, hbm, vmem, vmem],
        out_specs=vmem,
        scratch_shapes=[
            pltpu.VMEM((chunks - ready, half, depth), acts.dtype),
            pltpu.SemaphoreType.DMA((chunks - ready,)),
        ],
        compiler_params=medium,
        cost_estimate=cost,
    )(at, acts, out_grads, weights, early)
    order = tuple(range(pairs - 1, 0, -1))
    own, *coded = pl.pallas_call(
        functools.partial(code, order),
        out_shape=(pltpu.VMEM((lanes, tokens), jnp.float32),)
        + (pltpu.VMEM((lanes + 16, tokens), jnp.int16),) * (pairs - 1),
        in_specs=[smem, vmem, vmem],
        out_specs=(vmem,) * pairs,
        compiler_params=small,
    )(at, kept, got)
    parts = [
        lax.ppermute(block, "tensor", [(i, i ^ (2 * m)) for i in range(split)])
        for m, block in zip(order, coded)
    ]
    lives = pl.pallas_call(
        functools.partial(members, pairs),
        out_shape=pltpu.VMEM((owners, tokens), jnp.float32),
        in_specs=[smem] * 3,
        out_specs=vmem,
        compiler_params=small,
    )(doc_lengths, owner_map, at)
    grads = pl.pallas_call(
        outer,
        out_shape=pltpu.VMEM((owners, rank // 2, lanes), jnp.float32),
        in_specs=[vmem] * (pairs + 1),
        out_specs=vmem,
        scratch_shapes=[
            pltpu.VMEM((rank, tokens), jnp.float32),
            pltpu.VMEM((owners * rank // 2, 6 * tokens), jnp.bfloat16),
            pltpu.VMEM((lanes, 6 * tokens), jnp.bfloat16),
        ],
        compiler_params=small,
    )(lives, own, *parts)
    got = lax.all_to_all(
        grads.reshape(owners * rank // 2, lanes), ("dp", "tensor"), 0, 0, tiled=True
    )
    blocks = rank * rank // (split * lanes)
    return jnp.sum(got.reshape(owners, split, blocks, lanes), 1).reshape(owners, blocks * lanes)


def solution(mesh):
    in_specs = (
        P("dp", "tensor"),
        P("dp", "tensor"),
        P("tensor", None),
        P("tensor", None),
        P("dp", None),
        P("dp", None),
    )
    out_specs = P("dp", "tensor")
    return jax.shard_map(
        on_device, mesh=mesh, in_specs=in_specs, out_specs=out_specs, check_vma=False
    )
```
